32 devices in a mesh: ctx: 8 (over y, x, core), grp: 4 (over z).
Axes of the slice: x: 2, y: 2, z: 4, core: 2. Of those that a mesh axis runs over, the one named last changes fastest.
Arguments:
- residual: bfloat16 [4, 1024, 2880], P('grp', 'ctx'), may hold values from -3 to 3
- queries: bfloat16 [4, 1024, 2048], P('grp', 'ctx'), may hold values from -8 to 8
- stretch_kv: bfloat16 [4, 1024, 1024], P('grp', 'ctx'), may hold values from -8 to 8
- cache_kv: bfloat16 [4, 2048, 1024], P('grp', 'ctx'), may hold values from -6 to 6
- doc_lengths: int32 [4, 8], P('grp'), may hold values from 1 to 1536, 3072 in all within a row
- sinks: float32 [32], replicated, may hold values from 2 to 6
- out_proj: bfloat16 [2048, 2880], P('ctx'), may hold values from -0.75 to 0.75
- norm_gain: float32 [2880], replicated, may hold values from 0.1 to 1.9
- router: bfloat16 [2880, 16], replicated, may hold values from -0.109375 to 0.109375
- expert_ids: int32 [4, 1024, 4], P('grp', 'ctx'), may hold values from 0 to 15, all different within a row; in each aligned block of 128 rows (0 to 127, 128 to 255, ..., all dimensions but the last counted through in order) at most 40 rows name the same one
- expert_in: bfloat16 [32, 2880, 1536], P(('ctx', 'grp')), may hold values from -0.109375 to 0.109375
- expert_out: bfloat16 [32, 768, 2880], P(('ctx', 'grp')), may hold values from -0.15625 to 0.15625
Outputs:
- resid_mid: bfloat16 [4, 1024, 2880], P('grp', 'ctx')
- layer_out: bfloat16 [4, 1024, 2880], P('grp', 'ctx')
The draws below stay inside these ranges and needn't reach their ends.
Inputs may be any that keep to these rules, and one draw needn't show every extreme that they name: `expert_ids`: in the rows of one device (aligned blocks of 128 tokens, sequence after sequence), each expert is named by at most 40 rows, and in some blocks one expert by exactly 40; a token's 4 experts differ. `doc_lengths`: A sequence's 8 lengths sum to 3072; the longest is exactly 1536.
All inputs are finite; a program needn't handle non-finite values.
Results may differ from the reference program's by a relative error of at most 0.015.
Values may be sent and summed in bfloat16 or wider, within the bound.
A program may use at most 128 MiB of HBM per device.

```python
import math
import jax
import jax.numpy as jnp
import numpy as np
from jax import lax

D = 2880
HEADS = 32
KVH = 8
HD = 64
EXP_HID = 1536
HALF = 768
TOPK = 4
NDOCS = 8
TOK_DEV = 128
SEQS = 4
STRETCH = 1024
CACHE = 2048
LENGTH = 3072
EXPERTS = 16
OWNERS = 32
CAP = 40
N_CTX = 8
N_GRP = 4


def draw_queries(key, part):
    shape = (SEQS, STRETCH, HEADS * HD)
    values = jax.random.truncated_normal(jax.random.fold_in(key, 11), -6.0, 6.0, shape, jnp.float32)
    return values.astype(jnp.bfloat16)


def draw_stretch_kv(key, part):
    shape = (SEQS, STRETCH, 2 * KVH * HD)
    values = jax.random.truncated_normal(jax.random.fold_in(key, 21), -6.0, 6.0, shape, jnp.float32)
    return values.astype(jnp.bfloat16)


def steps_of(own_key, shape, split, smallest, high):
    def one(dim, parts):
        steps = jax.random.uniform(jax.random.fold_in(jax.random.fold_in(own_key, 6), dim), (parts,), jnp.float32, smallest / len(split), high / len(split))
        return jnp.repeat(jnp.exp(steps), shape[dim] // parts).reshape((-1,) + (1,) * (len(shape) - dim - 1))

    level = one(*split[0])
    for cut in split[1:]:
        level = level * one(*cut)
    return level


def split_up(count, total, most, slope):
    loads = [(1 << 20) // math.isqrt(grade ** slope) + 1 for grade in range(2, count + 1)]
    spare, given = total - most - (count - 1), [1] * (count - 1)
    while spare > 0:
        free = [i for i in range(count - 1) if given[i] < most]
        whole, remaining = sum([loads[i] for i in free]), spare
        for i in free:
            more = min(most - given[i], max(1, remaining * loads[i] // whole), spare)
            given[i] = given[i] + more
            spare = spare - more
    return np.array([most] + given)


def uneven_parts(key, amount, total, limit, skew):
    if amount == 2:
        one = jax.random.randint(key, (), max(1, total - limit), min(limit, total - 1) + 1)
        return jnp.stack([one, total - one])
    sizes = jnp.asarray(split_up(amount, total, limit, skew), jnp.int32)
    pairs = (amount - 1) // 2
    donor, sink = sizes[1:1 + 2 * pairs:2], sizes[2:2 + 2 * pairs:2]
    slack = jnp.minimum(donor - 1, limit - sink)
    shifted = jax.random.randint(jax.random.fold_in(key, 1), (pairs,), 0, 1 << 20) % (slack + 1)
    sizes = sizes.at[1:1 + 2 * pairs:2].set(donor - shifted).at[2:2 + 2 * pairs:2].set(sink + shifted)
    return sizes[jax.random.permutation(jax.random.fold_in(key, 2), amount)]


def routed_block(own_key, own, number, rows, number_of, top, limit, lean):
    order = jax.random.permutation(own_key, number_of)
    heavy_load, ordinary = shares(number_of, rows * top, limit, lean, True), shares(number_of, rows * top, limit, lean, False)
    places = jnp.arange(number_of)

    def named(tallies, turn):
        used = int((tallies > 0).sum())
        fixed = max(1, used // 4)
        shifted = fixed + (places - fixed + turn * (used - fixed)) % max(1, number_of - fixed)
        return jnp.zeros((number_of,), jnp.int32).at[order[jnp.where(places < fixed, places, shifted)]].set(jnp.asarray(tallies, jnp.int32))

    tallies = jnp.where(number % 4 == 0, named(heavy_load, number // 4), named(ordinary, number - number // 4 - 1))
    mixed = jax.random.permutation(jax.random.fold_in(own, 3), number_of)
    source_of, sink = mixed[0:number_of // 2 * 2:2], mixed[1:number_of // 2 * 2:2]
    margin = jnp.minimum(tallies[source_of] - 1, limit - tallies[sink]) // 2
    margin = jnp.where((source_of == order[0]) | (sink == order[0]) | (tallies[sink] == 0), 0, jnp.maximum(margin, 0))
    shifted = jax.random.randint(jax.random.fold_in(own, 4), (number_of // 2,), 0, 1 << 20) % (margin + 1)
    tallies = tallies.at[source_of].add(-shifted).at[sink].add(shifted)
    items = jnp.searchsorted(jnp.cumsum(tallies), jnp.arange(rows * top), side="right").astype(jnp.int32)
    listing = items.reshape(top, rows).T
    listing = listing[jax.random.permutation(jax.random.fold_in(own, 1), rows)]
    turn = jax.random.randint(jax.random.fold_in(own, 2), (rows, 1), 0, top)
    return jnp.take_along_axis(listing, (jnp.arange(top)[None, :] + turn) % top, axis=1)


def shares(number_of, total, reach, skew, full):
    weights = [(1 << 20) // math.isqrt(grade ** skew) + 1 for grade in range(1, number_of + 1)]
    largest = reach if full else min(reach, max(-(-total // number_of), total * weights[0] // sum(weights)))
    least = 1 if total - largest >= number_of - 1 else 0
    holding, spare = [largest] + [least] * (number_of - 1), total - largest - least * (number_of - 1)
    while spare > 0:
        movable = [i for i in range(1, number_of) if holding[i] < largest] or [i for i in range(1, number_of) if holding[i] < reach]
        whole, left = sum([weights[i] for i in movable]), spare
        for i in movable:
            addition = min(reach - holding[i], max(1, left * weights[i] // whole), spare)
            holding[i] = holding[i] + addition
            spare = spare - addition
    return np.array(holding)


def bell_draw(key, extent, width, most, shards=(), kind=jnp.bfloat16):
    loudness = steps_of(key, extent, shards, -0.22, 0.18) if shards else 1.0
    drawn = jax.random.normal(key, extent, jnp.float32) * width * loudness
    return jnp.minimum(jnp.maximum(drawn, -most), most).astype(kind)


def setup_inputs(seed: int = 0) -> dict:
    key_list = jax.random.split(jax.random.key(seed), 13)
    residual = bell_draw(key_list[0], (SEQS, STRETCH, D), 0.5, 3.0, ((0, 4), (1, 8)))
    queries = draw_queries(jax.random.fold_in(key_list[12], 71), 0)
    stretch_kv = draw_stretch_kv(jax.random.fold_in(key_list[12], 71), 0)
    cache_kv = bell_draw(key_list[3], (SEQS, CACHE, 2 * KVH * HD), 1.0, 6.0, ((0, 4), (1, 8)))
    doc_lengths = jax.vmap(lambda own: uneven_parts(own, NDOCS, LENGTH, LENGTH // 2, 1))(jax.random.split(key_list[4], SEQS)).reshape((SEQS, NDOCS)).astype(jnp.int32)
    sinks = jnp.clip(jax.random.uniform(key_list[5], (HEADS,), jnp.float32, 2.0, 6.0), 2.0, 6.0)
    out_proj = bell_draw(key_list[6], (HEADS * HD, D), 0.125, 0.75, ((0, 8),))
    norm_gain = jnp.clip(1.0 + 0.18 * jax.random.normal(key_list[7], (D,), jnp.float32), 0.1, 1.9)
    router = bell_draw(key_list[8], (D, EXPERTS), D ** -0.5, 0.109375)
    expert_ids_keys = jax.random.split(jax.random.fold_in(key_list[9], 1), SEQS * STRETCH // TOK_DEV)
    expert_ids_turns = jax.random.permutation(jax.random.fold_in(key_list[9], 3), SEQS * STRETCH // TOK_DEV)
    expert_ids = jax.vmap(lambda own, number: routed_block(jax.random.fold_in(key_list[9], 2), own, number, TOK_DEV, EXPERTS, TOPK, CAP, 1))(expert_ids_keys, expert_ids_turns).reshape((SEQS, STRETCH, TOPK))
    expert_in = bell_draw(key_list[10], (OWNERS, D, EXP_HID), D ** -0.5, 0.109375, ((0, 32),))
    expert_out = bell_draw(key_list[11], (OWNERS, HALF, D), EXP_HID ** -0.5, 0.15625, ((0, 32),))
    return dict(residual=residual, queries=queries, stretch_kv=stretch_kv, cache_kv=cache_kv, doc_lengths=doc_lengths, sinks=sinks, out_proj=out_proj, norm_gain=norm_gain, router=router, expert_ids=expert_ids, expert_in=expert_in, expert_out=expert_out)


def doc_index(positions, lengths):
    ends = jnp.cumsum(lengths)
    return lax.optimization_barrier(jnp.sum((positions[:, None] >= ends[None, :]).astype(jnp.int32), axis=1))

def gated_act(pre, half_width):
    gate = pre[:, :half_width]
    upper = pre[:, half_width:]
    return ((upper + 1.0) * gate * jax.nn.sigmoid(1.702 * gate)).astype(jnp.bfloat16)

def reference(residual, queries, stretch_kv, cache_kv, doc_lengths, sinks, out_proj, norm_gain, router, expert_ids, expert_in, expert_out):
    groups = HEADS // KVH
    kv_cols = KVH * HD
    block = math.gcd(STRETCH, 512)
    scale = 1.0 / math.sqrt(HD)
    sink_grid = sinks.reshape(KVH, groups).astype(jnp.float32)
    key_pos = jnp.arange(LENGTH, dtype=jnp.int32)

    def one_sequence(inputs):
        seq_queries, seq_stretch, seq_cache, seq_lengths = inputs
        joined = jnp.concatenate([seq_cache, seq_stretch], axis=0)
        keys = joined[:, :kv_cols].reshape(LENGTH, KVH, HD).astype(jnp.float32)
        values = joined[:, kv_cols:].reshape(LENGTH, KVH, HD).astype(jnp.float32)
        key_doc = doc_index(key_pos, seq_lengths)

        def one_block(index):
            first = (index * block).astype(jnp.int32)
            part = lax.dynamic_slice_in_dim(seq_queries, first, block, 0)
            part = part.reshape(block, KVH, groups, HD).astype(jnp.float32)
            query_pos = CACHE + first + jnp.arange(block, dtype=jnp.int32)
            query_doc = doc_index(query_pos, seq_lengths)
            allowed = (key_pos[None, :] <= query_pos[:, None]) & (key_doc[None, :] == query_doc[:, None])
            scores = jnp.einsum('qkgd,skd->kgqs', part, keys) * scale
            masked = jnp.where(allowed[None, None], scores, -jnp.inf)
            top = jnp.maximum(lax.optimization_barrier(jnp.max(masked, axis=-1)), sink_grid[:, :, None])
            weights = jnp.where(allowed[None, None], jnp.exp(scores - top[..., None]), 0.0)
            denom = lax.optimization_barrier(jnp.sum(weights, axis=-1)) + jnp.exp(sink_grid[:, :, None] - top)
            rounded = lax.optimization_barrier(weights.astype(jnp.bfloat16))
            numer = jnp.einsum('kgqs,skd->kgqd', rounded.astype(jnp.float32), values)
            result = numer / denom[..., None]
            return jnp.transpose(result, (2, 0, 1, 3)).reshape(block, HEADS * HD).astype(jnp.bfloat16)
        blocks = lax.map(one_block, jnp.arange(STRETCH // block, dtype=jnp.int32))
        return blocks.reshape(STRETCH, HEADS * HD)
    attended = lax.map(one_sequence, (queries, stretch_kv, cache_kv, doc_lengths))
    projected = jnp.dot(attended.reshape(-1, HEADS * HD), out_proj, preferred_element_type=jnp.float32)
    mid = (residual.reshape(-1, D).astype(jnp.float32) + projected).astype(jnp.bfloat16)
    mid_float = mid.astype(jnp.float32)
    normed = (mid_float * lax.rsqrt(lax.optimization_barrier(jnp.mean(mid_float * mid_float, axis=-1, keepdims=True)) + 1e-05) * norm_gain).astype(jnp.bfloat16)
    logits = jnp.dot(normed, router, preferred_element_type=jnp.float32)
    chosen_ids = expert_ids.reshape(-1, TOPK)
    picks = chosen_ids[:, :, None] == jnp.arange(EXPERTS, dtype=jnp.int32)[None, None, :]
    chosen = lax.optimization_barrier(jnp.sum(jnp.where(picks, logits[:, None, :], 0.0), axis=-1))
    raised = jnp.exp(chosen)
    route_weights = raised / lax.optimization_barrier(jnp.sum(raised, axis=-1, keepdims=True))
    flat_ids = chosen_ids.reshape(-1)
    weights_flat = route_weights.reshape(-1)
    most_rows = min(N_CTX * N_GRP * CAP, flat_ids.shape[0])

    def add_expert(index, total):
        order = jnp.argsort((flat_ids != index).astype(jnp.int32), stable=True)[:most_rows]
        token_rows = order // TOPK
        live = flat_ids[order] == index
        rows = normed[token_rows]
        summed = jnp.zeros((most_rows, D), jnp.float32)
        for half_index in range(2):
            owner = (2 * index + half_index).astype(jnp.int32)
            first_w = lax.dynamic_index_in_dim(expert_in, owner, 0, keepdims=False)
            second_w = lax.dynamic_index_in_dim(expert_out, owner, 0, keepdims=False)
            pre = jnp.dot(rows, first_w, preferred_element_type=jnp.float32)
            hidden = gated_act(pre, HALF)
            part_out = jnp.dot(hidden, second_w, preferred_element_type=jnp.float32).astype(jnp.bfloat16)
            summed = summed + part_out.astype(jnp.float32)
        rounded_rows = lax.optimization_barrier(summed.astype(jnp.bfloat16))
        contrib = rounded_rows.astype(jnp.float32) * jnp.where(live, weights_flat[order], 0.0)[:, None]
        return total.at[token_rows].add(contrib)
    mixture = lax.fori_loop(0, EXPERTS, add_expert, jnp.zeros((flat_ids.shape[0] // TOPK, D), jnp.float32))
    final = (mid_float + mixture).astype(jnp.bfloat16)
    return (mid.reshape(SEQS, STRETCH, D), final.reshape(SEQS, STRETCH, D))
```

```python
import functools
import math

import jax
import jax.numpy as jnp
from jax import lax
from jax.experimental import pallas as pl
from jax.experimental.pallas import tpu as pltpu
from jax.sharding import PartitionSpec as P

HEADS = 32
KVH = 8
HD = 64
KEY_BLOCK = 256
NEG = -1e30


def gated_act(pre, half_width):
    gate = pre[:, :half_width]
    upper = pre[:, half_width:]
    return ((upper + 1.0) * gate * jax.nn.sigmoid(1.702 * gate)).astype(jnp.bfloat16)


def attention_kernel(
    bounds, q_ref, cache_ref, stretch_ref, start_ref, sink_ref, out_ref, qs, top, total, acc
):
    tokens = q_ref.shape[0]
    pairs = KVH // 2
    per = 2 * (HEADS // KVH)
    kv_cols = KVH * HD
    cache_rows = cache_ref.shape[0]
    first_query = bounds[0]
    low = bounds[1]
    lane = lax.broadcasted_iota(jnp.int32, (tokens, 2 * HD), 1)
    lower = lane < HD
    for p in range(pairs):
        for j in range(0, per, 2):
            col = HD * (per * p + j)
            both = q_ref[:, col : col + 2 * HD].astype(jnp.float32) * (1.0 / math.sqrt(HD))
            turned = pltpu.roll(both, HD, 1)
            if j < per // 2:
                even = jnp.where(lower, both, 0.0)
                odd = jnp.where(lower, turned, 0.0)
            else:
                even = jnp.where(lower, 0.0, turned)
                odd = jnp.where(lower, 0.0, both)
            qs[p, j * tokens : (j + 1) * tokens, :] = even.astype(jnp.bfloat16)
            qs[p, (j + 1) * tokens : (j + 2) * tokens, :] = odd.astype(jnp.bfloat16)
    top[...] = sink_ref[...]
    total[...] = jnp.zeros_like(total)
    acc[...] = jnp.zeros_like(acc)
    starts = start_ref[...]
    query_pos = first_query + lax.broadcasted_iota(jnp.int32, (1, tokens), 1)

    def block(ref, row, base):
        row = pl.multiple_of(row, KEY_BLOCK)
        key_pos = base + row + lax.broadcasted_iota(jnp.int32, (KEY_BLOCK, tokens), 0)
        bias = jnp.where((key_pos >= starts) & (key_pos <= query_pos), 0.0, NEG)
        bias = jnp.concatenate([bias] * per, axis=1)
        for p in range(pairs):
            keys = ref[pl.ds(row, KEY_BLOCK), 2 * HD * p : 2 * HD * (p + 1)]
            values = ref[pl.ds(row, KEY_BLOCK), kv_cols + 2 * HD * p : kv_cols + 2 * HD * (p + 1)]
            scores = (
                lax.dot_general(
                    keys, qs[p], (((1,), (1,)), ((), ())), preferred_element_type=jnp.float32
                )
                + bias
            )
            old = top[p]
            new = jnp.maximum(old, jnp.max(scores, axis=0, keepdims=True))
            weights = jnp.exp(scores - new)
            shrink = jnp.exp(old - new)
            total[p] = total[p] * shrink + jnp.sum(weights, axis=0, keepdims=True)
            acc[p] = acc[p] * shrink + lax.dot_general(
                values,
                weights.astype(jnp.bfloat16),
                (((0,), (0,)), ((), ())),
                preferred_element_type=jnp.float32,
            )
            top[p] = new

    cache_blocks = cache_rows // KEY_BLOCK

    def cache_step(i, carry):
        block(cache_ref, i * KEY_BLOCK, 0)
        return carry

    def stretch_step(i, carry):
        block(stretch_ref, i * KEY_BLOCK, cache_rows)
        return carry

    lax.fori_loop(lax.div(low, KEY_BLOCK), cache_blocks, cache_step, 0)
    lax.fori_loop(
        lax.div(jnp.maximum(low - cache_rows, 0), KEY_BLOCK),
        lax.div(first_query + tokens - 1 - cache_rows, KEY_BLOCK) + 1,
        stretch_step,
        0,
    )
    for p in range(pairs):
        denom = total[p] + jnp.exp(sink_ref[p] - top[p])
        ready = acc[p] / denom
        for j in range(0, per, 2):
            row = 0 if j < per // 2 else HD
            upper = ready[row : row + HD, j * tokens : (j + 1) * tokens]
            under = ready[row : row + HD, (j + 1) * tokens : (j + 2) * tokens]
            col = HD * (per * p + j)
            out_ref[:, col : col + 2 * HD] = jnp.concatenate([upper, under], axis=0).T.astype(
                out_ref.dtype
            )


def attention(queries, cache_all, stretch_all, lengths, sinks, first_query):
    tokens = queries.shape[0]
    pairs = KVH // 2
    per = 2 * (HEADS // KVH)
    ends = jnp.cumsum(lengths)
    positions = first_query + jnp.arange(tokens, dtype=jnp.int32)
    starts = jnp.max(jnp.where(positions[:, None] >= ends[None, :], ends[None, :], 0), axis=1)
    bounds = jnp.stack([first_query, starts[0]]).astype(jnp.int32)
    sink_rows = jnp.repeat(sinks, tokens).reshape(pairs, 1, per * tokens)
    vmem = pl.BlockSpec(memory_space=pltpu.VMEM)
    return pl.pallas_call(
        attention_kernel,
        out_shape=jax.ShapeDtypeStruct(queries.shape, jnp.bfloat16),
        in_specs=[pl.BlockSpec(memory_space=pltpu.SMEM)] + [vmem] * 5,
        out_specs=vmem,
        scratch_shapes=[
            pltpu.VMEM((pairs, per * tokens, 2 * HD), jnp.bfloat16),
            pltpu.VMEM((pairs, 1, per * tokens), jnp.float32),
            pltpu.VMEM((pairs, 1, per * tokens), jnp.float32),
            pltpu.VMEM((pairs, 2 * HD, per * tokens), jnp.float32),
        ],
        compiler_params=pltpu.CompilerParams(vmem_limit_bytes=48 * 1024 * 1024),
        cost_estimate=pl.CostEstimate(
            flops=8_000_000_000, bytes_accessed=8_000_000, transcendentals=8_000_000
        ),
    )(bounds, queries, cache_all, stretch_all, starts[None, :].astype(jnp.int32), sink_rows)


def body(
    residual,
    queries,
    stretch_kv,
    cache_kv,
    doc_lengths,
    sinks,
    out_proj,
    norm_gain,
    router,
    expert_ids,
    expert_in,
    expert_out,
):
    tokens = residual.shape[1]
    width = residual.shape[2]
    cache_rows = cache_kv.shape[1]
    ctx_count = lax.axis_size("ctx")
    grp_count = lax.axis_size("grp")
    ctx_here = lax.axis_index("ctx")
    grp_here = lax.axis_index("grp")
    experts = router.shape[1]
    topk = expert_ids.shape[2]
    first_query = cache_rows * ctx_count + ctx_here * tokens
    cache_all = lax.all_gather(cache_kv[0], "ctx", axis=0, tiled=True)
    stretch_all = lax.all_gather(stretch_kv[0], "ctx", axis=0, tiled=True)
    proj_all = lax.all_gather(out_proj, "ctx", axis=0, tiled=True)
    ids_all = lax.all_gather(expert_ids[0], "grp", axis=0)

    plane_experts = (jnp.arange(ctx_count, dtype=jnp.int32) * grp_count + grp_here) // 2
    capacity = 2 * ((5 * tokens * topk + 8 * experts - 1) // (8 * experts))
    named = ids_all[..., None] == plane_experts
    hits = jnp.any(named, axis=2)
    before = jnp.tril(jnp.ones((tokens, tokens), jnp.bfloat16), -1)
    slots = jnp.einsum(
        "ut,gtc->guc", before, hits.astype(jnp.bfloat16), preferred_element_type=jnp.float32
    ).astype(jnp.int32)
    slots = jnp.where(hits, slots, -1)
    places = jnp.transpose(slots, (0, 2, 1))[:, :, None, :] == jnp.arange(
        capacity, dtype=jnp.int32
    )[None, None, :, None]
    places = places.reshape(grp_count, ctx_count * capacity, tokens).astype(jnp.bfloat16)

    attended = attention(
        queries[0], cache_all, stretch_all, doc_lengths[0], sinks, first_query
    )
    projected = jnp.dot(attended, proj_all, preferred_element_type=jnp.float32)
    mid = (residual[0].astype(jnp.float32) + projected).astype(jnp.bfloat16)
    mid_float = mid.astype(jnp.float32)
    normed = (
        mid_float
        * lax.rsqrt(jnp.mean(mid_float * mid_float, axis=-1, keepdims=True) + 1e-05)
        * norm_gain
    ).astype(jnp.bfloat16)
    column = lax.all_gather(normed, "grp", axis=0)
    logits = jnp.einsum("gtd,de->gte", column, router, preferred_element_type=jnp.float32)
    picks = ids_all[..., None] == jnp.arange(experts, dtype=jnp.int32)
    chosen = jnp.sum(jnp.where(picks, logits[:, :, None, :], 0.0), axis=-1)
    raised = jnp.exp(chosen)
    route_weights = raised / jnp.sum(raised, axis=-1, keepdims=True)
    by_expert = jnp.sum(jnp.where(named, route_weights[..., None], 0.0), axis=2)

    packed = jnp.einsum("gst,gtd->gsd", places, column, preferred_element_type=jnp.float32).astype(
        jnp.bfloat16
    )
    packed = jnp.transpose(packed.reshape(grp_count, ctx_count, capacity, width), (1, 0, 2, 3))
    received = lax.all_to_all(packed, "ctx", split_axis=0, concat_axis=0, tiled=True)
    in_weights = expert_in[0]
    out_weights = expert_out[0]
    pre = jnp.dot(received.reshape(-1, width), in_weights, preferred_element_type=jnp.float32)
    hidden = gated_act(pre, out_weights.shape[0])
    partial_out = jnp.dot(hidden, out_weights, preferred_element_type=jnp.float32).astype(
        jnp.bfloat16
    )
    returned = lax.all_to_all(
        partial_out.reshape(received.shape), "ctx", split_axis=0, concat_axis=0, tiled=True
    )
    places = places.reshape(grp_count, ctx_count, capacity, tokens)
    weighted = places.astype(jnp.float32) * jnp.transpose(by_expert, (0, 2, 1))[:, :, None, :]
    coarse = weighted.astype(jnp.bfloat16)
    fine = (weighted - coarse.astype(jnp.float32)).astype(jnp.bfloat16)
    mixture = jnp.einsum(
        "gcrt,cgrd->gtd", coarse, returned, preferred_element_type=jnp.float32
    ) + jnp.einsum("gcrt,cgrd->gtd", fine, returned, preferred_element_type=jnp.float32)
    sums = lax.psum_scatter(mixture.astype(jnp.bfloat16), "grp", scatter_dimension=0)
    final = (mid_float + sums.astype(jnp.float32)).astype(jnp.bfloat16)
    return (mid[None], final[None])


def solution(mesh):
    return jax.shard_map(
        body,
        mesh=mesh,
        in_specs=(
            P("grp", "ctx", None),
            P("grp", "ctx", None),
            P("grp", "ctx", None),
            P("grp", "ctx", None),
            P("grp", None),
            P(),
            P("ctx", None),
            P(),
            P(),
            P("grp", "ctx", None),
            P(("ctx", "grp"), None, None),
            P(("ctx", "grp"), None, None),
        ),
        out_specs=(P("grp", "ctx", None), P("grp", "ctx", None)),
        check_vma=False,
    )
```

```python
import functools
import math

import jax
import jax.numpy as jnp
from jax import lax
from jax.experimental import pallas as pl
from jax.experimental.pallas import tpu as pltpu
from jax.sharding import PartitionSpec as P

HEADS = 32
KVH = 8
HD = 64
KEY_BLOCK = 256
NEG = -1e30


def gated_act(pre, half_width):
    gate = pre[:, :half_width]
    upper = pre[:, half_width:]
    return ((upper + 1.0) * gate * jax.nn.sigmoid(1.702 * gate)).astype(jnp.bfloat16)


def attention_kernel(
    cache_rows, stretch_rows, lows, recv_ref, start_ref, sink_ref, out_ref, qs, top, total, acc
):
    sources = recv_ref.shape[0]
    span = cache_rows + stretch_rows
    tokens = stretch_rows
    heads = sink_ref.shape[1] // tokens
    cache_total = sources * cache_rows
    lower = lax.broadcasted_iota(jnp.int32, (tokens, 2 * HD), 1) < HD
    cache_per = KEY_BLOCK // cache_rows
    stretch_per = KEY_BLOCK // stretch_rows

    def query_block(b, carry):
        for j in range(0, heads, 2):
            first = span + j // 2 * tokens
            both = recv_ref[b, first : first + tokens, :].astype(jnp.float32)
            both = both * (1.0 / math.sqrt(HD))
            even = jnp.where(lower, both, 0.0)
            odd = jnp.where(lower, pltpu.roll(both, HD, 1), 0.0)
            qs[j * tokens : (j + 1) * tokens, :] = even.astype(jnp.bfloat16)
            qs[(j + 1) * tokens : (j + 2) * tokens, :] = odd.astype(jnp.bfloat16)
        top[...] = sink_ref[...]
        total[...] = jnp.zeros_like(total)
        acc[...] = jnp.zeros_like(acc)
        starts = start_ref[b]
        query_pos = cache_total + b * tokens + lax.broadcasted_iota(jnp.int32, (1, tokens), 1)
        low = lows[b]

        def block(keys_values, base):
            key_pos = base + lax.broadcasted_iota(jnp.int32, (KEY_BLOCK, tokens), 0)
            bias = jnp.where((key_pos >= starts) & (key_pos <= query_pos), 0.0, NEG)
            bias = jnp.concatenate([bias, bias], axis=1)
            for j in range(0, heads, 2):
                cols = slice(j * tokens, (j + 2) * tokens)
                scores = (
                    lax.dot_general(
                        keys_values,
                        qs[cols, :],
                        (((1,), (1,)), ((), ())),
                        preferred_element_type=jnp.float32,
                    )
                    + bias
                )
                old = top[:, cols]
                new = jnp.maximum(old, jnp.max(scores, axis=0, keepdims=True))
                weights = jnp.exp(scores - new)
                shrink = jnp.exp(old - new)
                total[:, cols] = total[:, cols] * shrink + jnp.sum(weights, axis=0, keepdims=True)
                acc[:, cols] = acc[:, cols] * shrink + lax.dot_general(
                    keys_values,
                    weights.astype(jnp.bfloat16),
                    (((0,), (0,)), ((), ())),
                    preferred_element_type=jnp.float32,
                )
                top[:, cols] = new

        def cache_step(i, inner):
            parts = [recv_ref[i * cache_per + k, :cache_rows, :] for k in range(cache_per)]
            block(jnp.concatenate(parts, axis=0), i * KEY_BLOCK)
            return inner

        def stretch_step(i, inner):
            parts = [
                recv_ref[i * stretch_per + k, cache_rows:span, :] for k in range(stretch_per)
            ]
            block(jnp.concatenate(parts, axis=0), cache_total + i * KEY_BLOCK)
            return inner

        lax.fori_loop(lax.div(low, KEY_BLOCK), cache_total // KEY_BLOCK, cache_step, 0)
        lax.fori_loop(
            lax.div(jnp.maximum(low - cache_total, 0), KEY_BLOCK),
            lax.div(b * tokens + tokens - 1, KEY_BLOCK) + 1,
            stretch_step,
            0,
        )
        denom = total[...] + jnp.exp(sink_ref[...] - top[...])
        ready = acc[HD:, :] / denom
        for j in range(0, heads, 2):
            pair = jnp.concatenate(
                [ready[:, j * tokens : (j + 1) * tokens], ready[:, (j + 1) * tokens : (j + 2) * tokens]],
                axis=0,
            )
            out_ref[b, :, j * HD : (j + 2) * HD] = pair.T.astype(out_ref.dtype)
        return carry

    lax.fori_loop(0, sources, query_block, 0)


def attention(queries, stretch_kv, cache_kv, lengths, sinks, ctx_here, ctx_count):
    tokens = queries.shape[0]
    cache_rows = cache_kv.shape[0]
    heads = HEADS // ctx_count
    local = jnp.concatenate([cache_kv, stretch_kv], axis=0)
    span = local.shape[0]
    local = local.reshape(span, 2, KVH, HD).transpose(2, 0, 1, 3).reshape(KVH, span, 2 * HD)
    local = jnp.repeat(local, ctx_count // KVH, axis=0)
    asked = queries.reshape(tokens, ctx_count, heads // 2, 2 * HD).transpose(1, 2, 0, 3)
    asked = asked.reshape(ctx_count, heads // 2 * tokens, 2 * HD)
    sent = jnp.concatenate([local, asked], axis=1)
    recv = lax.all_to_all(sent, "ctx", split_axis=0, concat_axis=0, tiled=True)
    ends = jnp.cumsum(lengths)
    positions = cache_rows * ctx_count + jnp.arange(ctx_count * tokens, dtype=jnp.int32)
    starts = jnp.max(jnp.where(positions[:, None] >= ends[None, :], ends[None, :], 0), axis=1)
    starts = starts.astype(jnp.int32).reshape(ctx_count, 1, tokens)
    own_sinks = lax.dynamic_slice_in_dim(sinks, ctx_here * heads, heads, 0)
    sink_row = jnp.repeat(own_sinks, tokens)[None, :]
    vmem = pl.BlockSpec(memory_space=pltpu.VMEM)
    attended = pl.pallas_call(
        functools.partial(attention_kernel, cache_rows, tokens),
        out_shape=jax.ShapeDtypeStruct((ctx_count, tokens, heads * HD), jnp.bfloat16),
        in_specs=[pl.BlockSpec(memory_space=pltpu.SMEM)] + [vmem] * 3,
        out_specs=vmem,
        scratch_shapes=[
            pltpu.VMEM((heads * tokens, 2 * HD), jnp.bfloat16),
            pltpu.VMEM((1, heads * tokens), jnp.float32),
            pltpu.VMEM((1, heads * tokens), jnp.float32),
            pltpu.VMEM((2 * HD, heads * tokens), jnp.float32),
        ],
        compiler_params=pltpu.CompilerParams(vmem_limit_bytes=32 * 1024 * 1024),
        cost_estimate=pl.CostEstimate(
            flops=8_000_000_000, bytes_accessed=2_000_000, transcendentals=8_000_000
        ),
    )(starts[:, 0, 0], recv, starts, sink_row)
    back = lax.all_to_all(attended, "ctx", split_axis=0, concat_axis=0, tiled=True)
    return back.transpose(1, 0, 2).reshape(tokens, HEADS * HD)


def body(
    residual,
    queries,
    stretch_kv,
    cache_kv,
    doc_lengths,
    sinks,
    out_proj,
    norm_gain,
    router,
    expert_ids,
    expert_in,
    expert_out,
):
    tokens = residual.shape[1]
    width = residual.shape[2]
    ctx_count = lax.axis_size("ctx")
    grp_count = lax.axis_size("grp")
    ctx_here = lax.axis_index("ctx")
    grp_here = lax.axis_index("grp")
    experts = router.shape[1]
    topk = expert_ids.shape[2]
    proj_all = lax.all_gather(out_proj, "ctx", axis=0, tiled=True)
    ids_all = lax.all_gather(expert_ids[0], "grp", axis=0)

    plane_experts = (jnp.arange(ctx_count, dtype=jnp.int32) * grp_count + grp_here) // 2
    capacity = 2 * ((5 * tokens * topk + 8 * experts - 1) // (8 * experts))
    named = ids_all[..., None] == plane_experts
    hits = jnp.any(named, axis=2)
    before = jnp.tril(jnp.ones((tokens, tokens), jnp.bfloat16), -1)
    slots = jnp.einsum(
        "ut,gtc->guc", before, hits.astype(jnp.bfloat16), preferred_element_type=jnp.float32
    ).astype(jnp.int32)
    slots = jnp.where(hits, slots, -1)
    places = jnp.transpose(slots, (0, 2, 1))[:, :, None, :] == jnp.arange(
        capacity, dtype=jnp.int32
    )[None, None, :, None]
    places = jnp.transpose(
        places.reshape(grp_count, ctx_count, capacity, tokens), (1, 0, 2, 3)
    )
    same = jnp.eye(grp_count, dtype=jnp.bool_)[None, :, None, :, None]
    spread = (places[:, :, :, None, :] & same).reshape(-1, grp_count * tokens)

    attended = attention(
        queries[0], stretch_kv[0], cache_kv[0], doc_lengths[0], sinks, ctx_here, ctx_count
    )
    projected = jnp.dot(attended, proj_all, preferred_element_type=jnp.float32)
    mid = (residual[0].astype(jnp.float32) + projected).astype(jnp.bfloat16)
    mid_float = mid.astype(jnp.float32)
    normed = (
        mid_float
        * lax.rsqrt(jnp.mean(mid_float * mid_float, axis=-1, keepdims=True) + 1e-05)
        * norm_gain
    ).astype(jnp.bfloat16)
    column = lax.all_gather(normed, "grp", axis=0)
    logits = jnp.einsum("gtd,de->gte", column, router, preferred_element_type=jnp.float32)
    picks = ids_all[..., None] == jnp.arange(experts, dtype=jnp.int32)
    chosen = jnp.sum(jnp.where(picks, logits[:, :, None, :], 0.0), axis=-1)
    raised = jnp.exp(chosen)
    route_weights = raised / jnp.sum(raised, axis=-1, keepdims=True)
    by_expert = jnp.sum(jnp.where(named, route_weights[..., None], 0.0), axis=2)

    packed = jnp.dot(
        spread.astype(jnp.bfloat16),
        column.reshape(-1, width),
        preferred_element_type=jnp.float32,
    ).astype(jnp.bfloat16)
    packed = packed.reshape(ctx_count, grp_count * capacity, width)
    received = lax.all_to_all(packed, "ctx", split_axis=0, concat_axis=0, tiled=True)
    in_weights = expert_in[0]
    out_weights = expert_out[0]
    pre = jnp.dot(received.reshape(-1, width), in_weights, preferred_element_type=jnp.float32)
    hidden = gated_act(pre, out_weights.shape[0])
    partial_out = jnp.dot(hidden, out_weights, preferred_element_type=jnp.float32).astype(
        jnp.bfloat16
    )
    returned = lax.all_to_all(
        partial_out.reshape(received.shape), "ctx", split_axis=0, concat_axis=0, tiled=True
    )
    scale = jnp.transpose(by_expert, (2, 0, 1))[:, :, None, :]
    weighted = jnp.where(places, scale, 0.0).astype(jnp.bfloat16)[:, :, :, None, :]
    weighted = jnp.where(same, weighted, jnp.zeros_like(weighted)).reshape(spread.shape)
    mixture = lax.dot_general(
        weighted,
        returned.reshape(-1, width),
        (((0,), (0,)), ((), ())),
        preferred_element_type=jnp.float32,
    ).reshape(grp_count, tokens, width)
    sums = lax.psum_scatter(mixture.astype(jnp.bfloat16), "grp", scatter_dimension=0)
    final = (mid_float + sums.astype(jnp.float32)).astype(jnp.bfloat16)
    return (mid[None], final[None])


def solution(mesh):
    return jax.shard_map(
        body,
        mesh=mesh,
        in_specs=(
            P("grp", "ctx", None),
            P("grp", "ctx", None),
            P("grp", "ctx", None),
            P("grp", "ctx", None),
            P("grp", None),
            P(),
            P("ctx", None),
            P(),
            P(),
            P("grp", "ctx", None),
            P(("ctx", "grp"), None, None),
            P(("ctx", "grp"), None, None),
        ),
        out_specs=(P("grp", "ctx", None), P("grp", "ctx", None)),
        check_vma=False,
    )
```

```python
import functools
import math

import jax
import jax.numpy as jnp
from jax import lax
from jax.experimental import pallas as pl
from jax.experimental.pallas import tpu as pltpu
from jax.sharding import PartitionSpec as P

HEADS = 32
KVH = 8
HD = 64
KEY_BLOCK = 256
NEG = -1e30


def gated_act(pre, half_width):
    gate = pre[:, :half_width]
    upper = pre[:, half_width:]
    return ((upper + 1.0) * gate * jax.nn.sigmoid(1.702 * gate)).astype(jnp.bfloat16)


def attention_kernel(
    cache_rows, stretch_rows, lows, recv_ref, start_ref, sink_ref, out_ref, qs, top, total, acc
):
    sources = recv_ref.shape[0]
    span = cache_rows + stretch_rows
    tokens = stretch_rows
    heads = sink_ref.shape[1] // tokens
    cache_total = sources * cache_rows
    lower = lax.broadcasted_iota(jnp.int32, (tokens, 2 * HD), 1) < HD
    cache_per = KEY_BLOCK // cache_rows
    stretch_per = KEY_BLOCK // stretch_rows

    def query_block(b, carry):
        for j in range(0, heads, 2):
            first = span + j // 2 * tokens
            both = recv_ref[b, first : first + tokens, :].astype(jnp.float32)
            both = both * (1.0 / math.sqrt(HD))
            even = jnp.where(lower, both, 0.0)
            odd = jnp.where(lower, pltpu.roll(both, HD, 1), 0.0)
            qs[j * tokens : (j + 1) * tokens, :] = even.astype(jnp.bfloat16)
            qs[(j + 1) * tokens : (j + 2) * tokens, :] = odd.astype(jnp.bfloat16)
        top[...] = sink_ref[...]
        total[...] = jnp.zeros_like(total)
        acc[...] = jnp.zeros_like(acc)
        starts = start_ref[b]
        query_pos = cache_total + b * tokens + lax.broadcasted_iota(jnp.int32, (1, tokens), 1)
        low = lows[b]

        def block(keys_values, base):
            key_pos = base + lax.broadcasted_iota(jnp.int32, (KEY_BLOCK, tokens), 0)
            bias = jnp.where((key_pos >= starts) & (key_pos <= query_pos), 0.0, NEG)
            bias = jnp.concatenate([bias, bias], axis=1)
            for j in range(0, heads, 2):
                cols = slice(j * tokens, (j + 2) * tokens)
                scores = (
                    lax.dot_general(
                        keys_values,
                        qs[cols, :],
                        (((1,), (1,)), ((), ())),
                        preferred_element_type=jnp.float32,
                    )
                    + bias
                )
                old = top[:, cols]
                new = jnp.maximum(old, jnp.max(scores, axis=0, keepdims=True))
                weights = jnp.exp(scores - new)
                shrink = jnp.exp(old - new)
                total[:, cols] = total[:, cols] * shrink + jnp.sum(weights, axis=0, keepdims=True)
                acc[:, cols] = acc[:, cols] * shrink + lax.dot_general(
                    keys_values,
                    weights.astype(jnp.bfloat16),
                    (((0,), (0,)), ((), ())),
                    preferred_element_type=jnp.float32,
                )
                top[:, cols] = new

        def cache_step(i, inner):
            parts = [recv_ref[i * cache_per + k, :cache_rows, :] for k in range(cache_per)]
            block(jnp.concatenate(parts, axis=0), i * KEY_BLOCK)
            return inner

        def stretch_step(i, inner):
            parts = [
                recv_ref[i * stretch_per + k, cache_rows:span, :] for k in range(stretch_per)
            ]
            block(jnp.concatenate(parts, axis=0), cache_total + i * KEY_BLOCK)
            return inner

        lax.fori_loop(lax.div(low, KEY_BLOCK), cache_total // KEY_BLOCK, cache_step, 0)
        lax.fori_loop(
            lax.div(jnp.maximum(low - cache_total, 0), KEY_BLOCK),
            lax.div(b * tokens + tokens - 1, KEY_BLOCK) + 1,
            stretch_step,
            0,
        )
        denom = total[...] + jnp.exp(sink_ref[...] - top[...])
        ready = acc[HD:, :] / denom
        for j in range(0, heads, 2):
            pair = jnp.concatenate(
                [ready[:, j * tokens : (j + 1) * tokens], ready[:, (j + 1) * tokens : (j + 2) * tokens]],
                axis=0,
            )
            out_ref[b, :, j * HD : (j + 2) * HD] = pair.T.astype(out_ref.dtype)
        return carry

    lax.fori_loop(0, sources, query_block, 0)


def attention(queries, stretch_kv, cache_kv, lengths, sinks, ctx_here, ctx_count):
    tokens = queries.shape[0]
    cache_rows = cache_kv.shape[0]
    heads = HEADS // ctx_count
    local = jnp.concatenate([cache_kv, stretch_kv], axis=0)
    span = local.shape[0]
    local = local.reshape(span, 2, KVH, HD).transpose(2, 0, 1, 3).reshape(KVH, span, 2 * HD)
    local = jnp.repeat(local, ctx_count // KVH, axis=0)
    asked = queries.reshape(tokens, ctx_count, heads // 2, 2 * HD).transpose(1, 2, 0, 3)
    asked = asked.reshape(ctx_count, heads // 2 * tokens, 2 * HD)
    sent = jnp.concatenate([local, asked], axis=1)
    recv = lax.all_to_all(sent, "ctx", split_axis=0, concat_axis=0, tiled=True)
    ends = jnp.cumsum(lengths)
    positions = cache_rows * ctx_count + jnp.arange(ctx_count * tokens, dtype=jnp.int32)
    starts = jnp.max(jnp.where(positions[:, None] >= ends[None, :], ends[None, :], 0), axis=1)
    starts = starts.astype(jnp.int32).reshape(ctx_count, 1, tokens)
    own_sinks = lax.dynamic_slice_in_dim(sinks, ctx_here * heads, heads, 0)
    sink_row = jnp.repeat(own_sinks, tokens)[None, :]
    vmem = pl.BlockSpec(memory_space=pltpu.VMEM)
    attended = pl.pallas_call(
        functools.partial(attention_kernel, cache_rows, tokens),
        out_shape=jax.ShapeDtypeStruct((ctx_count, tokens, heads * HD), jnp.bfloat16),
        in_specs=[pl.BlockSpec(memory_space=pltpu.SMEM)] + [vmem] * 3,
        out_specs=vmem,
        scratch_shapes=[
            pltpu.VMEM((heads * tokens, 2 * HD), jnp.bfloat16),
            pltpu.VMEM((1, heads * tokens), jnp.float32),
            pltpu.VMEM((1, heads * tokens), jnp.float32),
            pltpu.VMEM((2 * HD, heads * tokens), jnp.float32),
        ],
        compiler_params=pltpu.CompilerParams(vmem_limit_bytes=32 * 1024 * 1024),
        cost_estimate=pl.CostEstimate(
            flops=8_000_000_000, bytes_accessed=2_000_000, transcendentals=8_000_000
        ),
    )(starts[:, 0, 0], recv, starts, sink_row)
    back = lax.all_to_all(attended, "ctx", split_axis=0, concat_axis=0, tiled=True)
    return back.transpose(1, 0, 2).reshape(tokens, HEADS * HD)


def body(
    residual,
    queries,
    stretch_kv,
    cache_kv,
    doc_lengths,
    sinks,
    out_proj,
    norm_gain,
    router,
    expert_ids,
    expert_in,
    expert_out,
):
    tokens = residual.shape[1]
    width = residual.shape[2]
    ctx_count = lax.axis_size("ctx")
    grp_count = lax.axis_size("grp")
    ctx_here = lax.axis_index("ctx")
    grp_here = lax.axis_index("grp")
    experts = router.shape[1]
    topk = expert_ids.shape[2]
    proj_all = lax.all_gather(out_proj, "ctx", axis=0, tiled=True)
    ids_all = lax.all_gather(expert_ids[0], "grp", axis=0)

    plane_experts = (jnp.arange(ctx_count, dtype=jnp.int32) * grp_count + grp_here) // 2
    capacity = 2 * ((5 * tokens * topk + 8 * experts - 1) // (8 * experts))
    named = ids_all[..., None] == plane_experts
    hits = jnp.any(named, axis=2)
    before = jnp.tril(jnp.ones((tokens, tokens), jnp.bfloat16), -1)
    slots = jnp.einsum(
        "ut,gtc->guc", before, hits.astype(jnp.bfloat16), preferred_element_type=jnp.float32
    ).astype(jnp.int32)
    slots = jnp.where(hits, slots, -1)
    places = jnp.transpose(slots, (0, 2, 1))[:, :, None, :] == jnp.arange(
        capacity, dtype=jnp.int32
    )[None, None, :, None]
    places = jnp.transpose(
        places.reshape(grp_count, ctx_count, capacity, tokens), (1, 0, 2, 3)
    )
    same = jnp.eye(grp_count, dtype=jnp.bool_)[None, :, None, :, None]
    spread = (places[:, :, :, None, :] & same).reshape(-1, grp_count * tokens)

    attended = attention(
        queries[0], stretch_kv[0], cache_kv[0], doc_lengths[0], sinks, ctx_here, ctx_count
    )
    projected = jnp.dot(attended, proj_all, preferred_element_type=jnp.float32)
    mid = (residual[0].astype(jnp.float32) + projected).astype(jnp.bfloat16)
    mid_float = mid.astype(jnp.float32)
    normed = (
        mid_float
        * lax.rsqrt(jnp.mean(mid_float * mid_float, axis=-1, keepdims=True) + 1e-05)
        * norm_gain
    ).astype(jnp.bfloat16)
    cuts = ((0, width // 256 * 128 + 128), (width // 256 * 128 + 128, width))
    columns = [lax.all_gather(normed[:, lo:hi], "grp", axis=0) for lo, hi in cuts]
    column = jnp.concatenate(columns, axis=2)
    logits = jnp.einsum("gtd,de->gte", column, router, preferred_element_type=jnp.float32)
    picks = ids_all[..., None] == jnp.arange(experts, dtype=jnp.int32)
    chosen = jnp.sum(jnp.where(picks, logits[:, :, None, :], 0.0), axis=-1)
    raised = jnp.exp(chosen)
    route_weights = raised / jnp.sum(raised, axis=-1, keepdims=True)
    by_expert = jnp.sum(jnp.where(named, route_weights[..., None], 0.0), axis=2)

    packing = spread.astype(jnp.bfloat16)

    def exchange(rows):
        blocks = rows.astype(jnp.bfloat16).reshape(ctx_count, grp_count * capacity, -1)
        moved = lax.all_to_all(blocks, "ctx", split_axis=0, concat_axis=0, tiled=True)
        return moved.reshape(rows.shape)

    received = [
        exchange(
            jnp.dot(packing, c.reshape(-1, c.shape[2]), preferred_element_type=jnp.float32)
        )
        for c in columns
    ]
    in_weights = expert_in[0]
    out_weights = expert_out[0]
    pre = sum(
        jnp.dot(r, in_weights[lo:hi], preferred_element_type=jnp.float32)
        for r, (lo, hi) in zip(received, cuts)
    )
    hidden = gated_act(pre, out_weights.shape[0])
    returned = [
        exchange(jnp.dot(hidden, out_weights[:, lo:hi], preferred_element_type=jnp.float32))
        for lo, hi in cuts
    ]
    scale = jnp.transpose(by_expert, (2, 0, 1))[:, :, None, :]
    weighted = jnp.where(places, scale, 0.0).astype(jnp.bfloat16)[:, :, :, None, :]
    weighted = jnp.where(same, weighted, jnp.zeros_like(weighted)).reshape(spread.shape)
    sums = []
    for part in returned:
        mixture = lax.dot_general(
            weighted, part, (((0,), (0,)), ((), ())), preferred_element_type=jnp.float32
        ).reshape(grp_count, tokens, -1)
        sums.append(lax.psum_scatter(mixture.astype(jnp.bfloat16), "grp", scatter_dimension=0))
    sums = jnp.concatenate(sums, axis=1)
    final = (mid_float + sums.astype(jnp.float32)).astype(jnp.bfloat16)
    return (mid[None], final[None])


def solution(mesh):
    return jax.shard_map(
        body,
        mesh=mesh,
        in_specs=(
            P("grp", "ctx", None),
            P("grp", "ctx", None),
            P("grp", "ctx", None),
            P("grp", "ctx", None),
            P("grp", None),
            P(),
            P("ctx", None),
            P(),
            P(),
            P("grp", "ctx", None),
            P(("ctx", "grp"), None, None),
            P(("ctx", "grp"), None, None),
        ),
        out_specs=(P("grp", "ctx", None), P("grp", "ctx", None)),
        check_vma=False,
    )
```
